128 devices in a mesh: flow: 2 (over x_lo), gy: 64 (over z, x_hi, y, core).
Axes of the slice: x: 4 (x_hi: 2, x_lo: 2; x = x_hi * 2 + x_lo), y: 4, z: 4, core: 2. Of those that a mesh axis runs over, the one named last changes fastest.
Arguments:
- initial_state: float32 [32, 16, 32768], P('flow', None, 'gy'), may hold values from -6 to 6
- sources: float32 [32, 16, 32768], P('flow', None, 'gy'), may hold values from -6 to 6
- inverse: float32 [32, 16, 16, 32768], P('flow', None, None, 'gy'), may hold values from -0.0084 to 0.168
- couplings: float32 [3, 16, 16], replicated, may hold values from 0 to 3
Outputs:
- relaxed_state: float32 [32, 16, 32768], P('flow', None, 'gy')
The draws below stay inside these ranges and needn't reach their ends.
All inputs are finite; a program needn't handle non-finite values.
Results may differ from the reference program's by a relative error of at most 0.00018.
Values sent between devices are 32-bit elements; how exact they have to be, the bound alone decides.
No kernel may reach another device: no remote copies, remote signals or barrier semaphores. Data moves between devices by JAX's collectives and lax.ppermute only.
A program may use at most 192 MiB of HBM per device.

```python
import jax
import jax.numpy as jnp
from jax import lax

S = 16
BX = 16
JAC = 4
CZ = 32
NX = 32
CELLS = 32768


def coupling_diagonals(key):
    shared_key = jax.random.fold_in(key, 90)
    order_key, level_key = jax.random.split(shared_key)
    order = jax.random.permutation(order_key, jnp.arange(S, dtype=jnp.int32))
    leading = order % 3
    unit_draw = jax.random.uniform(level_key, (3, S), jnp.float32)
    strong_values = 2.5 + 0.5 * unit_draw
    weak_values = 0.05 + 0.05 * unit_draw
    direction = lax.broadcasted_iota(jnp.int32, (3, S), 0)
    return jnp.where(direction == leading[None, :], strong_values, weak_values)


def draw_initial_state(key, part):
    key = jax.random.fold_in(key, 14)
    level_key, rough_key = jax.random.split(key)
    shape = (NX, S, CELLS)
    levels = jax.random.uniform(level_key, (NX, S, 1), jnp.float32, -2.0, 2.0)
    rough_part = jnp.clip(jax.random.normal(rough_key, shape, jnp.float32), -4.0, 4.0)
    return rough_part + levels


def draw_sources(key, part):
    key = jax.random.fold_in(key, 11)
    shape = (NX, S, CELLS)
    return jnp.clip(jax.random.normal(key, shape, jnp.float32), -6.0, 6.0)


def draw_inverse(key, part):
    neighbour_diagonals = coupling_diagonals(key)
    key = jax.random.fold_in(key, 12)
    first_key, second_key = jax.random.split(key)
    shape = (NX, S, S, CELLS)
    weight_total = 2.0 * (neighbour_diagonals[0] + neighbour_diagonals[1] + neighbour_diagonals[2]) + 0.75
    margin = jax.random.uniform(first_key, (NX, S, 1, CELLS), jnp.float32, 1.01, 1.05)
    diagonal = 1.0 / (margin * weight_total[None, :, None, None])
    spread_part = jax.random.uniform(second_key, shape, jnp.float32, -0.05, 0.05) * diagonal
    on_diagonal = lax.broadcasted_iota(jnp.int32, shape, 1) == lax.broadcasted_iota(jnp.int32, shape, 2)
    return jnp.where(on_diagonal, jnp.broadcast_to(diagonal, shape), spread_part)


def draw_couplings(key, part):
    neighbour_diagonals = coupling_diagonals(key)
    key = jax.random.fold_in(key, 13)
    shape = (3, S, S)
    spread_part = jax.random.uniform(key, shape, jnp.float32, 0.0, 0.008)
    on_diagonal = lax.broadcasted_iota(jnp.int32, shape, 1) == lax.broadcasted_iota(jnp.int32, shape, 2)
    return jnp.where(on_diagonal, jnp.broadcast_to(neighbour_diagonals[:, :, None], shape), spread_part)


def setup_inputs(seed: int = 0) -> dict:
    key_of = jax.random.split(jax.random.key(seed), 5)
    return {
        "initial_state": draw_initial_state(jax.random.fold_in(key_of[4], 71), 0),
        "sources": draw_sources(jax.random.fold_in(key_of[4], 71), 0),
        "inverse": draw_inverse(jax.random.fold_in(key_of[4], 71), 0),
        "couplings": draw_couplings(jax.random.fold_in(key_of[4], 71), 0),
    }


def apply_coupling(matrix, values):
    return jnp.einsum("ts,psl->ptl", matrix, values, precision=lax.Precision.HIGHEST)


def z_neighbours(values):
    extent = values.shape[-1]
    z_position = lax.broadcasted_iota(jnp.int32, (extent,), 0) % CZ
    padded = jnp.pad(values, ((0, 0), (0, 0), (1, 1)))
    below_cells = jnp.where(z_position != 0, padded[..., :extent], jnp.zeros_like(values))
    above_cells = jnp.where(z_position != CZ - 1, padded[..., 2:], jnp.zeros_like(values))
    return below_cells + above_cells


def jacobi_step(values, y_padded, lower_plane, upper_plane, source_block, inverse_block, couplings):
    extent = values.shape[-1]
    stacked = jnp.concatenate([lower_plane[None], values, upper_plane[None]], 0)
    x_total = stacked[:-2] + stacked[2:]
    y_total = y_padded[..., :extent] + y_padded[..., 2 * CZ:]
    coupled = source_block + apply_coupling(couplings[0], x_total)
    coupled = coupled + apply_coupling(couplings[1], y_total)
    coupled = coupled + apply_coupling(couplings[2], z_neighbours(values))
    return jnp.sum(inverse_block * coupled[:, None], axis=2)


def relax_block(current_field, block_id, lower_plane, upper_plane, sources, inverse, couplings):
    first_plane = block_id * BX
    values = current_field[first_plane:first_plane + BX]
    source_block = sources[first_plane:first_plane + BX]
    inverse_block = inverse[first_plane:first_plane + BX]
    for step_id in range(JAC):
        y_padded = jnp.pad(values, ((0, 0), (0, 0), (CZ, CZ)))
        values = jacobi_step(values, y_padded, lower_plane, upper_plane, source_block, inverse_block, couplings)
    return current_field.at[first_plane:first_plane + BX].set(values)


def reference(initial_state, sources, inverse, couplings):
    block_count = NX // BX
    zero_plane = jnp.zeros((S, CELLS), jnp.float32)
    current_field = initial_state
    for block_id in range(block_count):
        first_plane = block_id * BX
        lower_plane = current_field[first_plane - 1] if block_id > 0 else zero_plane
        upper_plane = current_field[first_plane + BX] if block_id < block_count - 1 else zero_plane
        current_field = relax_block(current_field, block_id, lower_plane, upper_plane, sources, inverse, couplings)
    for block_id in reversed(range(block_count)):
        first_plane = block_id * BX
        lower_plane = current_field[first_plane - 1] if block_id > 0 else zero_plane
        upper_plane = current_field[first_plane + BX] if block_id < block_count - 1 else zero_plane
        current_field = relax_block(current_field, block_id, lower_plane, upper_plane, sources, inverse, couplings)
    return current_field
```

```python
import functools

import jax
import jax.numpy as jnp
from jax import lax
from jax.experimental import pallas as pl
from jax.experimental.pallas import tpu as pltpu
from jax.sharding import PartitionSpec as P

S = 16
BX = 16
CZ = 32
OWN = 512
T = 128
F32 = jnp.float32
BF16 = jnp.bfloat16

INV_ROWS = 6 * 256
SV0 = INV_ROWS
PAY1 = INV_ROWS + 18 * S
PAY2 = 3 * 256


def slot_iota(rows):
    return lax.broadcasted_iota(jnp.int32, (rows, T), 1) // CZ


def plane_of(flow, d):
    return jnp.where(flow == 1, d, BX - 1 - d)


def split_couplings(c):
    hi = c.astype(BF16)
    lo = (c - hi.astype(F32)).astype(BF16)
    return jnp.concatenate([hi, hi, lo], axis=1)


def mm(cb, v):
    hi = v.astype(BF16)
    lo = (v - hi.astype(F32)).astype(BF16)
    return jnp.dot(cb, jnp.concatenate([hi, lo, hi], axis=0), preferred_element_type=F32)


def z_masks(width):
    z = lax.broadcasted_iota(jnp.int32, (S, width), 1) % CZ
    return z != 0, z != CZ - 1


def yz_terms(u1, u2, masks):
    width = u1.shape[1]
    below, above = masks
    y = pltpu.roll(u1, CZ, 1) + pltpu.roll(u1, width - CZ, 1)
    z = jnp.where(below, pltpu.roll(u2, 1, 1), 0.0) + jnp.where(above, pltpu.roll(u2, width - 1, 1), 0.0)
    return y + z


def apply_inverse(pieces):
    out = []
    for get, c in pieces:
        acc = get(0) * c[0:1, :]
        for s in range(1, S):
            acc = acc + get(s) * c[s : s + 1, :]
        out.append(acc)
    return out


def low_high(slots, right, left):
    return jnp.where(slots < 2, right, left)


def pack_kernel(info, state, src, inv, pa1, pb1, pa2, pb2, g, ga, gb, edge, sem):
    flow, odd = info[0], info[1]

    def copy(i):
        d, side = i // 2, i % 2
        return pltpu.make_async_copy(
            inv.at[plane_of(flow, d), :, pl.ds(side * 384, T)], edge.at[i], sem.at[i]
        )

    for i in range(2 * BX):
        copy(i).start()
    slots = slot_iota(S)
    g[...] = state[plane_of(flow, 0)]
    for out1, out2, right in ((pa1, pa2, 1 - odd), (pb1, pb2, odd)):
        lane0 = pl.multiple_of(right * 384, T)
        row = SV0
        for d in range(BX):
            p = plane_of(flow, d)
            v = state[p, :, pl.ds(lane0, T)]
            r = src[p, :, pl.ds(lane0, T)]
            if d < 2:
                out1[row : row + S] = v
                out1[row + S : row + 2 * S] = r
                row += 2 * S
            else:
                keep = (slots < 2) == (right == 0)
                out1[row : row + S] = jnp.where(keep, v, pltpu.roll(r, 64, 1))
                row += S
    for out, right in ((ga, 1 - odd), (gb, odd)):
        out[...] = state[plane_of(flow, 0), :, pl.ds(pl.multiple_of(right * 384, T), T)]
    for i in range(2 * BX):
        copy(i).wait()
    slots8 = slot_iota(8)
    for out1, out2, right in ((pa1, pa2, 1 - odd), (pb1, pb2, odd)):
        for d in range(2):
            out1[d * 256 : (d + 1) * 256] = edge[2 * d + right]
        near = jnp.where(right == 1, 3, 0)
        next_ = jnp.where(right == 1, 2, 1)
        mask1 = [slots8 == ((near + q) & 3) for q in range(4)]
        mask2 = [slots8 == ((next_ + q) & 3) for q in range(4)]

        def rows(i, _, right=right, out1=out1, out2=out2, mask1=mask1, mask2=mask2):
            at = pl.multiple_of(i * 8, 8)
            for grp in range(3):
                one = two = jnp.zeros((8, T), F32)
                for q in range(4):
                    x = edge[2 * (2 + 4 * grp + q) + right, pl.ds(at, 8), :]
                    x = pltpu.roll(x, CZ * q, 1) if q else x
                    one = jnp.where(mask1[q], x, one)
                    two = jnp.where(mask2[q], x, two)
                out1[pl.ds((2 + grp) * 256 + at, 8), :] = one
                out2[pl.ds(grp * 256 + at, 8), :] = two
            keep = (slots8 < 2) == (right == 0)
            a = edge[28 + right, pl.ds(at, 8), :]
            b = edge[30 + right, pl.ds(at, 8), :]
            out1[pl.ds(5 * 256 + at, 8), :] = jnp.where(keep, a, pltpu.roll(b, 64, 1))
            return 0

        lax.fori_loop(0, 32, rows, 0, unroll=4)


def pack(info, state, src, inv):
    f = jax.ShapeDtypeStruct
    vm = pl.BlockSpec(memory_space=pltpu.VMEM)
    return pl.pallas_call(
        pack_kernel,
        in_specs=[pl.BlockSpec(memory_space=pltpu.SMEM), vm, vm, pl.BlockSpec(memory_space=pl.ANY)],
        out_specs=[vm] * 7,
        out_shape=[f((PAY1, T), F32)] * 2 + [f((PAY2, T), F32)] * 2 + [f((S, OWN), F32)] + [f((S, T), F32)] * 2,
        scratch_shapes=[pltpu.VMEM((2 * BX, 256, T), F32), pltpu.SemaphoreType.DMA((2 * BX,))],
        compiler_params=pltpu.CompilerParams(vmem_limit_bytes=24 * 2**20),
        name="pack",
    )(info, state, src, inv)


def turn_kernel(info, inv, out, buf, sem):
    flow = info[0]

    def copy(i):
        d, tile = i // 4, i % 4
        return pltpu.make_async_copy(
            inv.at[plane_of(flow, d), :, pl.ds(tile * T, T)], buf.at[i], sem.at[d]
        )

    for i in range(4 * BX):
        copy(i).start()
    for d in range(BX):
        for tile in range(4):
            copy(4 * d + tile).wait()
        for tile in range(4):
            for s in range(S):
                out[d, s, :, tile * T : (tile + 1) * T] = buf[4 * d + tile, pl.ds(s, S, stride=S), :]


def turn(info, inv):
    return pl.pallas_call(
        turn_kernel,
        in_specs=[pl.BlockSpec(memory_space=pltpu.SMEM), pl.BlockSpec(memory_space=pl.ANY)],
        out_specs=pl.BlockSpec(memory_space=pltpu.VMEM),
        out_shape=jax.ShapeDtypeStruct((BX, S, S, OWN), F32),
        scratch_shapes=[pltpu.VMEM((4 * BX, 256, T), F32), pltpu.SemaphoreType.DMA((BX,))],
        compiler_params=pltpu.CompilerParams(vmem_limit_bytes=40 * 2**20),
        name="turn",
    )(info, inv)


def all_planes(cb, width_in, width_out, near, v, u0, u12, src, own_inv, halo_inv, store):
    u0[0, :, :width_in] = jnp.zeros((S, width_in), F32) if near is None else mm(cb, near[:, :width_in])[:S]
    for d in range(BX):
        u = mm(cb, v[d, :, :width_in])
        u0[d + 1, :, :width_in] = u[:S]
        u12[d, :, :width_in] = u[S:]
    masks = z_masks(width_in)
    slots = slot_iota(S)
    for d in range(BX):
        c = yz_terms(u12[d, :S, :width_in], u12[d, S:, :width_in], masks) + u0[d, :, :width_in]
        if d + 1 < BX:
            c = c + u0[d + 2, :, :width_in]
        pieces = [(lambda s, d=d: own_inv[d, s], c[:, :OWN] + src[d, :, :OWN])]
        if width_out > OWN:
            ch = c[:, OWN : OWN + T]
            if width_in == OWN + 2 * T:
                ch = low_high(slots, ch, c[:, OWN + T :])
            pieces.append((lambda s, d=d: halo_inv[d, s], ch + src[d, :, OWN:]))
        for at, x in zip((0, OWN), apply_inverse(pieces)):
            store(d, at, x)


def crit_step(cb, planes, v, near_u0, src, own_inv, crit_inv, halo_inv):
    masks = z_masks(OWN + 2 * T)
    u = {d: mm(cb, x) for d, x in v.items()}
    out = {}
    for d in planes:
        parts = []
        if d in u:
            parts.append(yz_terms(u[d][S : 2 * S], u[d][2 * S :], masks))
        if d == 0:
            if near_u0 is not None:
                parts.append(near_u0)
        elif d - 1 in u:
            parts.append(u[d - 1][:S])
        if d + 1 in u:
            parts.append(u[d + 1][:S])
        if src is not None:
            parts.append(src(d))
        c = functools.reduce(lambda a, b: a + b, parts)

        def tile(side, d=d):
            return (lambda s: crit_inv[d, side, s]) if d < 2 else (lambda s: halo_inv[d, s])

        pieces = [(lambda s, d=d: own_inv[d, s], c[:, :OWN]), (tile(0), c[:, OWN : OWN + T]), (tile(1), c[:, OWN + T :])]
        out[d] = jnp.concatenate(apply_inverse(pieces), axis=1)
    return out


def sides(info, a, b):
    odd, first, last = info[1], info[2], info[3]
    right = jnp.where(odd == 1, b, a)
    left = jnp.where(odd == 1, a, b)
    return jnp.where(last == 1, 0.0, right), jnp.where(first == 1, 0.0, left)


def put_edges(info, plane_value, pa, pb, d):
    odd = info[1]
    low, high = plane_value[:, :T], plane_value[:, OWN - T : OWN]
    pa[d] = jnp.where(odd == 1, low, high)
    pb[d] = jnp.where(odd == 1, high, low)


def first_kernel(
    info, coup, state, src_in, own_inv, pa1, pb1, g, ga, gb,
    v2, ea, eb, g4, g4a, g4b, halo_inv, crit_inv, src,
    v, vc, sc, u0, u12,
):
    flow, odd, first, last = info[0], info[1], info[2], info[3]
    cb = split_couplings(coup[...])
    slots = slot_iota(S)

    for s in range(S):
        for d in range(2):
            r, l = sides(info, pa1[pl.ds(d * 256 + s, S, stride=S), :], pb1[pl.ds(d * 256 + s, S, stride=S), :])
            crit_inv[d, 0, s] = r
            crit_inv[d, 1, s] = l
            halo_inv[d, s] = low_high(slots, r, l)
    for grp in range(3):
        for s in range(S):
            at = (2 + grp) * 256 + s
            r, l = sides(info, pa1[pl.ds(at, S, stride=S), :], pb1[pl.ds(at, S, stride=S), :])
            for q in range(4):
                x = jnp.where(slots == q, r, jnp.where(slots == (q + 3) % 4, l, 0.0))
                halo_inv[2 + 4 * grp + q, s] = pltpu.roll(x, T - CZ * q, 1) if q else x
    for s in range(S):
        at = 5 * 256 + s
        r, l = sides(info, pa1[pl.ds(at, S, stride=S), :], pb1[pl.ds(at, S, stride=S), :])
        halo_inv[14, s] = low_high(slots, r, l)
        halo_inv[15, s] = pltpu.roll(low_high(slots, l, r), 64, 1)

    for d in range(BX):
        p = plane_of(flow, d)
        v[d, :, :OWN] = state[p]
        src[d, :, :OWN] = src_in[p]
        if d < 2:
            at = SV0 + 2 * S * d
            r, l = sides(info, pa1[at : at + S], pb1[at : at + S])
            vc[d, :, :T] = r
            vc[d, :, T:] = l
            v[d, :, OWN:] = low_high(slots, r, l)
            r, l = sides(info, pa1[at + S : at + 2 * S], pb1[at + S : at + 2 * S])
            sc[d, :, :T] = r
            sc[d, :, T:] = l
            src[d, :, OWN:] = low_high(slots, r, l)
        else:
            at = SV0 + 2 * S + S * d
            r, l = sides(info, pa1[at : at + S], pb1[at : at + S])
            v[d, :, OWN:] = low_high(slots, r, l)
            src[d, :, OWN:] = pltpu.roll(low_high(slots, l, r), 64, 1)

    g_right, g_left = sides(info, ga[...], gb[...])
    use = flow == 0

    @pl.when(use)
    def _():
        def wide(own, combined, tiles, d):
            if d < 2:
                return jnp.concatenate([own, tiles[d]], axis=1)
            return jnp.concatenate([own, combined, combined], axis=1)

        vals = {d: wide(v[d, :, :OWN], v[d, :, OWN:], vc, d) for d in range(5)}
        near = mm(cb, jnp.concatenate([g[...], g_right, g_left], axis=1))[:S]
        for k in range(1, 5):
            vals = crit_step(
                cb, range(5 - k), vals, near,
                lambda d: wide(src[d, :, :OWN], src[d, :, OWN:], sc, d),
                own_inv, crit_inv, halo_inv,
            )
        top = vals[0]
        g4[...] = top[:, :OWN]
        g4a[...] = jnp.where(odd == 1, top[:, :T], top[:, OWN - T : OWN])
        g4b[...] = jnp.where(odd == 1, top[:, OWN - T : OWN], top[:, :T])

    @pl.when(jnp.logical_not(use))
    def _():
        g4[...] = jnp.zeros((S, OWN), F32)
        g4a[...] = jnp.zeros((S, T), F32)
        g4b[...] = jnp.zeros((S, T), F32)

    near = jnp.concatenate([g[...], low_high(slots, g_right, g_left)], axis=1)
    near = jnp.where(use, near, 0.0)

    def keep(d, at, x):
        v[d, :, at : at + x.shape[1]] = x

    def final(d, at, x):
        v2[d] = x
        put_edges(info, x, ea, eb, d)

    all_planes(cb, 640, 640, near, v, u0, u12, src, own_inv, halo_inv, keep)
    all_planes(cb, 640, 512, near, v, u0, u12, src, own_inv, halo_inv, final)


def later_kernel(second, *refs):
    if second:
        (info, coup, v_in, ea_in, eb_in, own_inv, halo_inv, crit_inv, src, g, ga, gb, h, ha, hb, pa2, pb2,
         v_out, ea, eb, halo_out, v, u0, u12) = refs
    else:
        (info, coup, v_in, ea_in, eb_in, own_inv, halo_out, src, h, ha, hb,
         v_out, g8, g8a, g8b, v, u0, u12) = refs
    flow, odd = info[0], info[1]
    cb = split_couplings(coup[...])
    slots = slot_iota(S)
    for d in range(BX):
        v[d, :, :OWN] = v_in[d]
        r, l = sides(info, ea_in[d], eb_in[d])
        v[d, :, OWN : OWN + T] = r
        v[d, :, OWN + T :] = l

    if second:
        for d in (0, 1, 14, 15):
            halo_out[d] = halo_inv[d]
        for grp in range(3):
            for s in range(S):
                at = grp * 256 + s
                r, l = sides(info, pa2[pl.ds(at, S, stride=S), :], pb2[pl.ds(at, S, stride=S), :])
                for q in range(4):
                    d = 2 + 4 * grp + q
                    x = jnp.where(slots == (q + 1) % 4, r, jnp.where(slots == (q + 2) % 4, l, 0.0))
                    halo_out[d, s] = halo_inv[d, s] + (pltpu.roll(x, T - CZ * q, 1) if q else x)

    h_right, h_left = sides(info, ha[...], hb[...])
    h_wide = jnp.concatenate([h[...], h_right, h_left], axis=1)

    if second:
        @pl.when(flow == 1)
        def _():
            near = mm(cb, h_wide)[:S]
            d1 = crit_step(cb, range(1), {}, near, None, own_inv, crit_inv, halo_inv)
            d2 = crit_step(cb, range(2), d1, near, None, own_inv, crit_inv, halo_inv)
            for d in range(2):
                v[d] = v[d] + d2[d]

    h_wide = jnp.where(flow == 1, h_wide, 0.0)
    near = h_wide
    if second:
        g_right, g_left = sides(info, ga[...], gb[...])
        near = jnp.where(flow == 1, h_wide, jnp.concatenate([g[...], g_right, g_left], axis=1))

    def narrow(x):
        return jnp.concatenate([x[:, :OWN], low_high(slots, x[:, OWN : OWN + T], x[:, OWN + T :])], axis=1)

    def keep(d, at, x):
        v[d, :, at : at + x.shape[1]] = x

    def final(d, at, x):
        v_out[d] = x
        if second:
            put_edges(info, x, ea, eb, d)
        elif d == 0:
            g8[...] = x
            low, high = x[:, :T], x[:, OWN - T :]
            g8a[...] = jnp.where(odd == 1, low, high)
            g8b[...] = jnp.where(odd == 1, high, low)

    all_planes(cb, 768, 640, near, v, u0, u12, src, own_inv, halo_out, keep)
    all_planes(cb, 640, 640, narrow(near), v, u0, u12, src, own_inv, halo_out, keep)
    all_planes(cb, 640, 512, narrow(h_wide), v, u0, u12, src, own_inv, halo_out, final)


def last_kernel(info, coup, v8, own_inv, halo_inv, crit_inv, g8, g8a, g8b, out):
    flow = info[0]
    for d in range(BX):
        out[plane_of(flow, d)] = v8[d]

    @pl.when(flow == 0)
    def _():
        cb = split_couplings(coup[...])
        r, l = sides(info, g8a[...], g8b[...])
        near = mm(cb, jnp.concatenate([g8[...], r, l], axis=1))[:S]
        vals = {}
        for j in range(1, 5):
            vals = crit_step(cb, range(j), vals, near, None, own_inv, crit_inv, halo_inv)
        for d in range(4):
            p = BX - 1 - d
            out[p] = v8[d] + vals[d][:, :OWN]


def call(kernel, name, ins, outs, scratch, limit=48):
    f = jax.ShapeDtypeStruct
    vm = pl.BlockSpec(memory_space=pltpu.VMEM)
    return pl.pallas_call(
        kernel,
        in_specs=[pl.BlockSpec(memory_space=pltpu.SMEM)] + [vm] * (len(ins) - 1),
        out_specs=[vm] * len(outs),
        out_shape=[f(s, F32) for s in outs],
        scratch_shapes=[pltpu.VMEM(s, F32) for s in scratch],
        compiler_params=pltpu.CompilerParams(vmem_limit_bytes=limit * 2**20),
        name=name,
    )(*ins)


def shards(state, src_in, inverse, couplings):
    count = lax.axis_size("gy")
    flow = lax.axis_index("flow")
    at = lax.axis_index("gy")
    info = jnp.stack([flow, at % 2, at == 0, at == count - 1]).astype(jnp.int32)
    coup = couplings.reshape(3 * S, S)
    inv = inverse.reshape(BX, S * S, OWN)

    mate = [i ^ 1 for i in range(count)]
    other = [(i + 1) % count if i % 2 else (i - 1) % count for i in range(count)]

    def swap_a(x):
        return lax.ppermute(x, "gy", list(enumerate(mate)))

    def swap_b(x):
        return lax.ppermute(x, "gy", list(enumerate(other)))

    def cross(x, to):
        pairs = [(f * count + i, (1 - f) * count + to[i]) for f in (0, 1) for i in range(count)]
        return lax.ppermute(x, ("flow", "gy"), pairs)

    def swap_f(x):
        return lax.ppermute(x, "flow", [(0, 1), (1, 0)])

    def hop(x, xa, xb):
        return swap_f(x), cross(xa, mate), cross(xb, other)

    pa1, pb1, pa2, pb2, g, ga, gb = pack(info, state, src_in, inv)
    pb1, pa1 = swap_b(pb1), swap_a(pa1)
    g, ga, gb = hop(g, ga, gb)
    pb2, pa2 = swap_b(pb2), swap_a(pa2)
    own_inv = turn(info, inv)

    plane, tile, tiles = (S, OWN), (S, T), (BX, S, T)
    field = (BX, S, OWN)
    v2, ea, eb, h, ha, hb, halo, crit, src = call(
        first_kernel, "first",
        [info, coup, state, src_in, own_inv, pa1, pb1, g, ga, gb],
        [field, tiles, tiles, plane, tile, tile, (BX, S, S, T), (2, 2, S, S, T), (BX, S, 640)],
        [(BX, S, 640), (2, S, 2 * T), (2, S, 2 * T), (BX + 2, S, 640), (BX, 2 * S, 640)],
    )
    h, ha, hb = hop(h, ha, hb)
    eb, ea = swap_b(eb), swap_a(ea)
    wide = [(BX, S, 768), (BX + 2, S, 768), (BX, 2 * S, 768)]
    v5, ea, eb, halo = call(
        functools.partial(later_kernel, True), "second",
        [info, coup, v2, ea, eb, own_inv, halo, crit, src, g, ga, gb, h, ha, hb, pa2, pb2],
        [field, tiles, tiles, (BX, S, S, T)], wide,
    )
    eb, ea = swap_b(eb), swap_a(ea)
    v8, g8, g8a, g8b = call(
        functools.partial(later_kernel, False), "third",
        [info, coup, v5, ea, eb, own_inv, halo, src, h, ha, hb],
        [field, plane, tile, tile], wide,
    )
    g8, g8a, g8b = hop(g8, g8a, g8b)
    (out,) = call(
        last_kernel, "last", [info, coup, v8, own_inv, halo, crit, g8, g8a, g8b], [field], [],
    )
    return out


def solution(mesh):
    return jax.shard_map(
        shards,
        mesh=mesh,
        in_specs=(P("flow", None, "gy"), P("flow", None, "gy"), P("flow", None, None, "gy"), P()),
        out_specs=P("flow", None, "gy"),
        check_vma=False,
    )
```

```python
import functools

import jax
import jax.numpy as jnp
from jax import lax
from jax.experimental import pallas as pl
from jax.experimental.pallas import tpu as pltpu
from jax.sharding import PartitionSpec as P

S = 16
BX = 16
CZ = 32
OWN = 512
T = 128
F32 = jnp.float32
BF16 = jnp.bfloat16

SV0 = 6 * 256
PAY1 = SV0 + 18 * S
SV1 = 5 * 256
PAY2 = SV1 + 2 * S
PACK_LIMIT = 58
TURN_LIMIT = 40


def position():
    at = lax.axis_index("gy")
    return lax.axis_index("flow"), at % 2, at == 0, at == lax.axis_size("gy") - 1


def slot_iota(rows):
    return lax.broadcasted_iota(jnp.int32, (rows, T), 1) // CZ


def plane_of(flow, d):
    return jnp.where(flow == 1, d, BX - 1 - d)


def split_couplings(c):
    hi = c.astype(BF16)
    lo = (c - hi.astype(F32)).astype(BF16)
    return jnp.concatenate([hi, hi, lo], axis=1)


def mm(cb, v):
    hi = v.astype(BF16)
    lo = (v - hi.astype(F32)).astype(BF16)
    return jnp.dot(cb, jnp.concatenate([hi, lo, hi], axis=0), preferred_element_type=F32)


def z_masks(width):
    z = lax.broadcasted_iota(jnp.int32, (S, width), 1) % CZ
    return z != 0, z != CZ - 1


def yz_terms(u1, u2, masks):
    width = u1.shape[1]
    below, above = masks
    y = pltpu.roll(u1, CZ, 1) + pltpu.roll(u1, width - CZ, 1)
    z = jnp.where(below, pltpu.roll(u2, 1, 1), 0.0) + jnp.where(above, pltpu.roll(u2, width - 1, 1), 0.0)
    return y + z


def apply_inverse(pieces):
    out = []
    for get, c in pieces:
        acc = get(0) * c[0:1, :]
        for s in range(1, S):
            acc = acc + get(s) * c[s : s + 1, :]
        out.append(acc)
    return out


def low_high(slots, right, left):
    return jnp.where(slots < 2, right, left)


def pack_kernel(state, src, inv, pa1, pb1, pa2, pb2, edge, next1, se, re, s1, s2, sem, osem):
    flow, odd, _, _ = position()
    place = (1 - odd, odd)
    started = []

    def fetch(source, target):
        c = pltpu.make_async_copy(source, target, sem.at[len(started)])
        c.start()
        started.append(c)
        return c

    field = [fetch(x.at[:, :, pl.ds(384 * side, T)], y.at[side]) for x, y in ((state, se), (src, re)) for side in (0, 1)]
    planes = {}
    for d in range(2, BX):
        for side in (0, 1):
            planes[d, side] = fetch(inv.at[plane_of(flow, d), :, pl.ds(384 * side, T)], edge.at[2 * d - 4 + side])
    rest = []
    for side in (0, 1):
        at = pl.ds(384 * side, T)
        at2 = pl.ds(T + T * side, T)
        rest.append(fetch(inv.at[plane_of(flow, 1), :, at2], next1.at[side]))
        rest.append(fetch(inv.at[plane_of(flow, 0), :, at], s1.at[place[side], pl.ds(0, 256)]))
        rest.append(fetch(inv.at[plane_of(flow, 1), :, at], s1.at[place[side], pl.ds(256, 256)]))
        rest.append(fetch(inv.at[plane_of(flow, 0), :, at2], s2.at[place[side], pl.ds(0, 256)]))
        rest.append(fetch(src.at[plane_of(flow, 0), :, at2], s2.at[place[side], pl.ds(SV1, S)]))
    sent = []

    def send(scratch, outs, row, count):
        for j in range(2):
            c = pltpu.make_async_copy(
                scratch.at[j, pl.ds(row, count)], outs[j].at[pl.ds(row, count)], osem.at[len(sent)]
            )
            c.start()
            sent.append(c)

    for c in field:
        c.wait()
    slots = slot_iota(S)
    for side in (0, 1):
        j = place[side]
        row = SV0
        for d in range(BX):
            p = plane_of(flow, d)
            v, r = se[side, p], re[side, p]
            if d < 2:
                s1[j, row : row + S] = v
                s1[j, row + S : row + 2 * S] = r
                row += 2 * S
            else:
                s1[j, row : row + S] = jnp.where((slots >= 2) if side else (slots < 2), v, pltpu.roll(r, 64, 1))
                row += S
        s2[j, SV1 + S : SV1 + 2 * S] = re[side, plane_of(flow, 2)]
    send(s1, (pa1, pb1), SV0, 18 * S)

    slots8 = slot_iota(8)
    for grp in range(3):
        for q in range(4):
            for side in (0, 1):
                planes[2 + 4 * grp + q, side].wait()

        def rows(i, _, grp=grp):
            at = pl.multiple_of(i * 8, 8)
            for side in (0, 1):
                one = two = None
                for q in range(4):
                    x = edge[2 * (4 * grp + q) + side, pl.ds(at, 8), :]
                    x = pltpu.roll(x, CZ * q, 1) if q else x
                    one = x if one is None else jnp.where(slots8 == ((3 if side else 0) + q) % 4, x, one)
                    two = x if two is None else jnp.where(slots8 == ((2 if side else 1) + q) % 4, x, two)
                s1[place[side], pl.ds((2 + grp) * 256 + at, 8), :] = one
                s2[place[side], pl.ds((2 + grp) * 256 + at, 8), :] = two
            return 0

        lax.fori_loop(0, 32, rows, 0, unroll=8)
        send(s1, (pa1, pb1), (2 + grp) * 256, 256)
        send(s2, (pa2, pb2), (2 + grp) * 256, 256)
    for d in (14, 15):
        for side in (0, 1):
            planes[d, side].wait()
    for c in rest:
        c.wait()
    send(s1, (pa1, pb1), 0, 512)
    send(s2, (pa2, pb2), 0, 256)

    def rows(i, _):
        at = pl.multiple_of(i * 8, 8)
        for side in (0, 1):
            j = place[side]
            a = edge[24 + side, pl.ds(at, 8), :]
            b = edge[26 + side, pl.ds(at, 8), :]
            s1[j, pl.ds(5 * 256 + at, 8), :] = jnp.where((slots8 >= 2) if side else (slots8 < 2), a, pltpu.roll(b, 64, 1))
            s2[j, pl.ds(256 + at, 8), :] = jnp.where(
                slots8 == (3 if side else 0), next1[side, pl.ds(at, 8), :], edge[side, pl.ds(at, 8), :]
            )
        return 0

    lax.fori_loop(0, 32, rows, 0, unroll=8)
    send(s1, (pa1, pb1), 5 * 256, 256)
    send(s2, (pa2, pb2), 256, 256)
    send(s2, (pa2, pb2), SV1, 2 * S)
    for c in sent:
        c.wait()


def pack(state, src, inv):
    f = jax.ShapeDtypeStruct
    hbm = pl.BlockSpec(memory_space=pltpu.HBM)
    return pl.pallas_call(
        pack_kernel,
        in_specs=[hbm] * 3,
        out_specs=[hbm] * 4,
        out_shape=[f((PAY1, T), F32)] * 2 + [f((PAY2, T), F32)] * 2,
        scratch_shapes=[
            pltpu.VMEM((2 * BX - 4, 256, T), F32),
            pltpu.VMEM((2, 256, T), F32),
            pltpu.VMEM((2, BX, S, T), F32),
            pltpu.VMEM((2, BX, S, T), F32),
            pltpu.VMEM((2, PAY1, T), F32),
            pltpu.VMEM((2, PAY2, T), F32),
            pltpu.SemaphoreType.DMA((42,)),
            pltpu.SemaphoreType.DMA((24,)),
        ],
        compiler_params=pltpu.CompilerParams(vmem_limit_bytes=PACK_LIMIT * 2**20),
        name="pack",
    )(state, src, inv)


def turn_kernel(inv, out, buf, sem):
    flow = position()[0]

    def copy(i):
        d, tile = i // 4, i % 4
        return pltpu.make_async_copy(
            inv.at[plane_of(flow, d), :, pl.ds(tile * T, T)], buf.at[i], sem.at[d]
        )

    for i in range(4 * BX):
        copy(i).start()
    for d in range(BX):
        for tile in range(4):
            copy(4 * d + tile).wait()
        for tile in range(4):
            for s in range(S):
                out[d, s, :, tile * T : (tile + 1) * T] = buf[4 * d + tile, pl.ds(s, S, stride=S), :]


def turn(inv):
    return pl.pallas_call(
        turn_kernel,
        in_specs=[pl.BlockSpec(memory_space=pltpu.HBM)],
        out_specs=pl.BlockSpec(memory_space=pltpu.VMEM),
        out_shape=jax.ShapeDtypeStruct((BX, S, S, OWN), F32),
        scratch_shapes=[pltpu.VMEM((4 * BX, 256, T), F32), pltpu.SemaphoreType.DMA((BX,))],
        compiler_params=pltpu.CompilerParams(vmem_limit_bytes=TURN_LIMIT * 2**20),
        name="turn",
    )(inv)


def all_planes(cb, width_in, width_out, near, v, u0, u12, src, own_inv, halo_inv, store):
    u0[0, :, :width_in] = jnp.zeros((S, width_in), F32) if near is None else mm(cb, near[:, :width_in])[:S]
    for d in range(BX):
        u = mm(cb, v[d, :, :width_in])
        u0[d + 1, :, :width_in] = u[:S]
        u12[d, :, :width_in] = u[S:]
    masks = z_masks(width_in)
    slots = slot_iota(S)
    for d in range(BX):
        c = yz_terms(u12[d, :S, :width_in], u12[d, S:, :width_in], masks) + u0[d, :, :width_in]
        if d + 1 < BX:
            c = c + u0[d + 2, :, :width_in]
        pieces = [(lambda s, d=d: own_inv[d, s], c[:, :OWN] + src[d, :, :OWN])]
        if width_out > OWN:
            ch = c[:, OWN : OWN + T]
            if width_in == OWN + 2 * T:
                ch = low_high(slots, ch, c[:, OWN + T :])
            pieces.append((lambda s, d=d: halo_inv[d, s], ch + src[d, :, OWN:]))
        for at, x in zip((0, OWN), apply_inverse(pieces)):
            store(d, at, x)


def fit(x, width):
    have = x.shape[1]
    if have == width:
        return x
    side = (width - OWN) // 2
    return jnp.concatenate([x[:, : OWN + side], x[:, have - side :]], axis=1)


def crit_step(cb, planes, v, near_u0, src, inv, wide=()):
    u = {d: mm(cb, x) for d, x in v.items()}
    out = {}
    for d in planes:
        width = OWN + (4 if d in wide else 2) * T
        parts = []
        if d in u:
            masks = z_masks(u[d].shape[1])
            parts.append(yz_terms(u[d][S : 2 * S], u[d][2 * S :], masks))
        if d == 0:
            parts.append(near_u0)
        elif d - 1 in u:
            parts.append(u[d - 1][:S])
        if d + 1 in u:
            parts.append(u[d + 1][:S])
        if src is not None:
            parts.append(src(d))
        c = functools.reduce(lambda a, b: a + b, [fit(x, width) for x in parts])
        order = (0, 1, 2, -2, -1) if d in wide else (0, 1, -1)
        pieces = []
        at = 0
        for i in order:
            n = T if i else OWN
            pieces.append((inv(d, i), c[:, at : at + n]))
            at += n
        out[d] = jnp.concatenate(apply_inverse(pieces), axis=1)
    return out


def sides(a, b):
    _, odd, first, last = position()
    right = jnp.where(odd == 1, b, a)
    left = jnp.where(odd == 1, a, b)
    return jnp.where(last, 0.0, right), jnp.where(first, 0.0, left)


def put_edges(x, pa, pb, at, first=0, count=1):
    odd = position()[1]
    low = x[:, first * T : (first + count) * T]
    high = x[:, OWN - (first + count) * T : OWN - first * T]
    pa[at] = jnp.where(odd == 1, low, high)
    pb[at] = jnp.where(odd == 1, high, low)


def first_kernel(
    coup, state, src_in, own_inv, pa1, pb1, g, ga, gb,
    v2, ea, eb, h, ha, hb, halo_inv, crit_inv, src, sc,
    v, vc, u0, u12,
):
    flow = position()[0]
    cb = split_couplings(coup[...])
    slots = slot_iota(S)

    for s in range(S):
        for d in range(2):
            r, l = sides(pa1[pl.ds(d * 256 + s, S, stride=S), :], pb1[pl.ds(d * 256 + s, S, stride=S), :])
            crit_inv[d, 0, s] = r
            crit_inv[d, 1, s] = l
            halo_inv[d, s] = low_high(slots, r, l)
    for grp in range(3):
        for s in range(S):
            at = (2 + grp) * 256 + s
            r, l = sides(pa1[pl.ds(at, S, stride=S), :], pb1[pl.ds(at, S, stride=S), :])
            for q in range(4):
                x = jnp.where(slots == q, r, jnp.where(slots == (q + 3) % 4, l, 0.0))
                halo_inv[2 + 4 * grp + q, s] = pltpu.roll(x, T - CZ * q, 1) if q else x
    for s in range(S):
        at = 5 * 256 + s
        r, l = sides(pa1[pl.ds(at, S, stride=S), :], pb1[pl.ds(at, S, stride=S), :])
        halo_inv[14, s] = low_high(slots, r, l)
        halo_inv[15, s] = pltpu.roll(low_high(slots, l, r), 64, 1)

    for d in range(BX):
        p = plane_of(flow, d)
        v[d, :, :OWN] = state[p]
        src[d, :, :OWN] = src_in[p]
        if d < 2:
            at = SV0 + 2 * S * d
            r, l = sides(pa1[at : at + S], pb1[at : at + S])
            vc[d, :, :T] = r
            vc[d, :, T:] = l
            v[d, :, OWN:] = low_high(slots, r, l)
            r, l = sides(pa1[at + S : at + 2 * S], pb1[at + S : at + 2 * S])
            sc[d, :, :T] = r
            sc[d, :, T:] = l
            src[d, :, OWN:] = low_high(slots, r, l)
        else:
            at = SV0 + 2 * S + S * d
            r, l = sides(pa1[at : at + S], pb1[at : at + S])
            v[d, :, OWN:] = low_high(slots, r, l)
            src[d, :, OWN:] = pltpu.roll(low_high(slots, l, r), 64, 1)

    g_right, g_left = sides(ga[...], gb[...])
    use = flow == 0

    @pl.when(use)
    def _():
        def wide(own, combined, tiles, d):
            if d < 2:
                return jnp.concatenate([own, tiles[d]], axis=1)
            return jnp.concatenate([own, combined, combined], axis=1)

        def inv(d, i):
            if i == 0:
                return lambda s: own_inv[d, s]
            return (lambda s: crit_inv[d, int(i < 0), s]) if d < 2 else (lambda s: halo_inv[d, s])

        vals = {d: wide(v[d, :, :OWN], v[d, :, OWN:], vc, d) for d in range(5)}
        near = mm(cb, jnp.concatenate([g[...], g_right, g_left], axis=1))[:S]
        for k in range(1, 5):
            vals = crit_step(
                cb, range(5 - k), vals, near, lambda d: wide(src[d, :, :OWN], src[d, :, OWN:], sc, d), inv
            )
        top = vals[0][:, :OWN]
        h[...] = top
        put_edges(top, ha, hb, slice(None), 0, 2)

    @pl.when(jnp.logical_not(use))
    def _():
        h[...] = jnp.zeros((S, OWN), F32)
        ha[...] = jnp.zeros((S, 2 * T), F32)
        hb[...] = jnp.zeros((S, 2 * T), F32)

    near = jnp.concatenate([g[...], low_high(slots, g_right, g_left)], axis=1)
    near = jnp.where(use, near, 0.0)

    def keep(d, at, x):
        v[d, :, at : at + x.shape[1]] = x

    def final(d, at, x):
        v2[d] = x
        put_edges(x, ea, eb, d)
        if d < 2:
            put_edges(x, ea, eb, BX + d, 1)

    all_planes(cb, 640, 640, near, v, u0, u12, src, own_inv, halo_inv, keep)
    all_planes(cb, 640, 512, near, v, u0, u12, src, own_inv, halo_inv, final)


def load_field(v, v_in, ea_in, eb_in):
    for d in range(BX):
        v[d, :, :OWN] = v_in[d]
        r, l = sides(ea_in[d], eb_in[d])
        v[d, :, OWN : OWN + T] = r
        v[d, :, OWN + T :] = l


def narrow(x, slots):
    x = fit(x, OWN + 2 * T)
    return jnp.concatenate([x[:, :OWN], low_high(slots, x[:, OWN : OWN + T], x[:, OWN + T :])], axis=1)


def second_kernel(
    coup, v_in, ea_in, eb_in, own_inv, halo_in, crit_inv, src, g, ga, gb, h, ha, hb, pa2, pb2,
    v_out, ea, eb, halo_inv,
    v, u0, u12,
):
    flow = position()[0]
    cb = split_couplings(coup[...])
    slots = slot_iota(S)
    load_field(v, v_in, ea_in, eb_in)

    def taken(at):
        return sides(pa2[pl.ds(at, S, stride=S), :], pb2[pl.ds(at, S, stride=S), :])

    for d in (0, 1, 14, 15):
        halo_inv[d] = halo_in[d]
    for grp in range(3):
        for s in range(S):
            r, l = taken((2 + grp) * 256 + s)
            for q in range(4):
                d = 2 + 4 * grp + q
                x = jnp.where(slots == (q + 1) % 4, r, jnp.where(slots == (q + 2) % 4, l, 0.0))
                halo_inv[d, s] = halo_in[d, s] + (pltpu.roll(x, T - CZ * q, 1) if q else x)

    h_wide = jnp.concatenate([h[...], *sides(ha[...], hb[...])], axis=1)

    @pl.when(flow == 1)
    def _():
        def inv(d, i):
            return (lambda s: crit_inv[d, int(i < 0), s]) if i else (lambda s: own_inv[d, s])

        near = mm(cb, fit(h_wide, OWN + 2 * T))[:S]
        d1 = crit_step(cb, range(1), {}, near, None, inv)
        d2 = crit_step(cb, range(2), d1, near, None, inv)
        for d in range(2):
            v[d] = v[d] + d2[d]

    h_near = jnp.where(flow == 1, fit(h_wide, OWN + 2 * T), 0.0)
    g_wide = jnp.concatenate([g[...], *sides(ga[...], gb[...])], axis=1)
    near = jnp.where(flow == 1, h_near, g_wide)

    def keep(d, at, x):
        v[d, :, at : at + x.shape[1]] = x

    def final(d, at, x):
        v_out[d] = x
        put_edges(x, ea, eb, d)

    all_planes(cb, 768, 640, near, v, u0, u12, src, own_inv, halo_inv, keep)
    all_planes(cb, 640, 640, narrow(near, slots), v, u0, u12, src, own_inv, halo_inv, keep)
    all_planes(cb, 640, 512, narrow(h_near, slots), v, u0, u12, src, own_inv, halo_inv, final)


def cone_kernel(
    coup, v_in, ea_in, eb_in, own_inv, halo_inv, crit_inv, src, sc, h, ha, hb, pa2, pb2,
    g8, g8a, g8b,
    far, third,
):
    flow = position()[0]
    cb = split_couplings(coup[...])
    slots = slot_iota(S)

    def taken(at):
        return sides(pa2[pl.ds(at, S, stride=S), :], pb2[pl.ds(at, S, stride=S), :])

    h_wide = jnp.concatenate([h[...], *sides(ha[...], hb[...])], axis=1)

    @pl.when(flow == 1)
    def _():
        for s in range(S):
            far[0, 0, s], far[0, 1, s] = taken(s)
            r, l = taken(256 + s)
            far[1, 0, s] = jnp.where(slots == 0, r, 0.0)
            far[1, 1, s] = jnp.where(slots == 3, l, 0.0)
            third[0, s] = jnp.where(slots < 2, halo_inv[2, s], jnp.where(slots == 2, r, 0.0))
            third[1, s] = jnp.where(slots >= 2, halo_inv[2, s], jnp.where(slots == 1, l, 0.0))

        def inv(d, i):
            if i == 0:
                return lambda s: own_inv[d, s]
            if abs(i) == 2:
                return lambda s: far[d, int(i < 0), s]
            if d < 2:
                return lambda s: crit_inv[d, int(i < 0), s]
            return (lambda s: third[int(i < 0), s]) if d == 2 else (lambda s: halo_inv[d, s])

        near = mm(cb, h_wide)[:S]
        d1 = crit_step(cb, range(1), {}, near, None, inv, (0,))
        d2 = crit_step(cb, range(2), d1, near, None, inv, (0, 1))
        vals = {}
        for d in range(7):
            r, l = sides(ea_in[d], eb_in[d])
            if d < 2:
                r2, l2 = sides(ea_in[BX + d], eb_in[BX + d])
                vals[d] = jnp.concatenate([v_in[d], r, r2, l2, l], axis=1) + d2[d]
            else:
                vals[d] = jnp.concatenate([v_in[d], r, l], axis=1)

        def source(d):
            own = src[d, :, :OWN]
            if d > 2:
                return jnp.concatenate([own, src[d, :, OWN:], src[d, :, OWN:]], axis=1)
            if d == 2:
                return jnp.concatenate([own, *sides(pa2[SV1 + S : SV1 + 2 * S], pb2[SV1 + S : SV1 + 2 * S])], axis=1)
            if d == 1:
                return jnp.concatenate([own, sc[1]], axis=1)
            r, l = sides(pa2[SV1 : SV1 + S], pb2[SV1 : SV1 + S])
            return jnp.concatenate([own, sc[0, :, :T], r, l, sc[0, :, T:]], axis=1)

        for k in range(3, 9):
            vals = crit_step(cb, range(9 - k), vals, near, source, inv, (0,) if k == 3 else ())
        top = vals[0][:, :OWN]
        g8[...] = top
        put_edges(top, g8a, g8b, slice(None))

    @pl.when(flow == 0)
    def _():
        g8[...] = jnp.zeros((S, OWN), F32)
        g8a[...] = jnp.zeros((S, T), F32)
        g8b[...] = jnp.zeros((S, T), F32)


def third_kernel(
    coup, v_in, ea_in, eb_in, own_inv, halo_inv, crit_inv, src, h, ha, hb, g8, g8a, g8b,
    out,
    v, u0, u12, done, sem,
):
    flow = position()[0]
    cb = split_couplings(coup[...])
    slots = slot_iota(S)
    load_field(v, v_in, ea_in, eb_in)
    g_wide = jnp.concatenate([g8[...], *sides(g8a[...], g8b[...])], axis=1)

    @pl.when(flow == 0)
    def _():
        def inv(d, i):
            return (lambda s: crit_inv[d, int(i < 0), s]) if i else (lambda s: own_inv[d, s])

        v[0] = v[0] + crit_step(cb, range(1), {}, mm(cb, g_wide)[:S], None, inv)[0]

    h_wide = fit(jnp.concatenate([h[...], *sides(ha[...], hb[...])], axis=1), OWN + 2 * T)
    near = jnp.where(flow == 1, h_wide, g_wide)

    def keep(d, at, x):
        v[d, :, at : at + x.shape[1]] = x

    sent = []

    def final(d, at, x):
        done[d] = x
        c = pltpu.make_async_copy(done.at[d], out.at[plane_of(flow, d)], sem.at[d])
        c.start()
        sent.append(c)

    all_planes(cb, 768, 640, near, v, u0, u12, src, own_inv, halo_inv, keep)
    all_planes(cb, 640, 640, narrow(near, slots), v, u0, u12, src, own_inv, halo_inv, keep)
    all_planes(cb, 640, 512, narrow(near, slots), v, u0, u12, src, own_inv, halo_inv, final)
    for c in sent:
        c.wait()


def call(kernel, name, ins, outs, scratch, out_space=pltpu.VMEM, limit=16):
    f = jax.ShapeDtypeStruct
    vm = pl.BlockSpec(memory_space=pltpu.VMEM)
    return pl.pallas_call(
        kernel,
        in_specs=[vm] * len(ins),
        out_specs=[pl.BlockSpec(memory_space=out_space)] * len(outs),
        out_shape=[f(s, F32) for s in outs],
        scratch_shapes=[pltpu.VMEM(s, F32) if isinstance(s, tuple) else s for s in scratch],
        compiler_params=pltpu.CompilerParams(vmem_limit_bytes=limit * 2**20),
        name=name,
    )(*ins)


def shards(state, src_in, inverse, couplings):
    count = lax.axis_size("gy")
    flow = lax.axis_index("flow")
    at = lax.axis_index("gy")
    coup = couplings.reshape(3 * S, S)
    inv = inverse.reshape(BX, S * S, OWN)

    mate = [i ^ 1 for i in range(count)]
    other = [(i + 1) % count if i % 2 else (i - 1) % count for i in range(count)]

    def swap_a(x):
        return lax.ppermute(x, "gy", list(enumerate(mate)))

    def swap_b(x):
        return lax.ppermute(x, "gy", list(enumerate(other)))

    def cross(x, to):
        pairs = [(f * count + i, (1 - f) * count + to[i]) for f in (0, 1) for i in range(count)]
        return lax.ppermute(x, ("flow", "gy"), pairs)

    def swap_f(x):
        return lax.ppermute(x, "flow", [(0, 1), (1, 0)])

    def hop(x, xa, xb):
        return swap_f(x), cross(xa, mate), cross(xb, other)

    g = jnp.where(flow == 1, state[0], state[BX - 1])
    low, high = g[:, :T], g[:, OWN - T :]
    ga, gb = jnp.where(at % 2 == 1, low, high), jnp.where(at % 2 == 1, high, low)
    g, ga, gb = hop(g, ga, gb)
    pa1, pb1, pa2, pb2 = pack(state, src_in, inv)
    pb1, pa1 = swap_b(pb1), swap_a(pa1)
    own_inv = turn(inv)
    pa1, g, ga, gb, own_inv, pa2, pb2 = lax.optimization_barrier((pa1, g, ga, gb, own_inv, pa2, pb2))
    pb2, pa2 = swap_b(pb2), swap_a(pa2)

    plane, tile, tiles = (S, OWN), (S, T), (BX, S, T)
    field = (BX, S, OWN)
    v2, ea, eb, h, ha, hb, halo, crit, src, sc = call(
        first_kernel, "first",
        [coup, state, src_in, own_inv, pa1, pb1, g, ga, gb],
        [field, (BX + 2, S, T), (BX + 2, S, T), plane, (S, 2 * T), (S, 2 * T), (BX, S, S, T), (2, 2, S, S, T),
         (BX, S, 640), (2, S, 2 * T)],
        [(BX, S, 640), (2, S, 2 * T), (BX + 2, S, 640), (BX, 2 * S, 640)],
    )
    h, ha, hb, ea, eb, pa2 = lax.optimization_barrier((h, ha, hb, ea, eb, pa2))
    eb, ea = swap_b(eb), swap_a(ea)
    h, ha = swap_f(h), cross(ha, mate)
    ea, hb = lax.optimization_barrier((ea, hb))
    hb = cross(hb, other)
    wide = [(BX, S, 768), (BX + 2, S, 768), (BX, 2 * S, 768)]
    v5, ea5, eb5, halo = call(
        second_kernel, "second",
        [coup, v2, ea, eb, own_inv, halo, crit, src, g, ga, gb, h, ha, hb, pa2, pb2],
        [field, tiles, tiles, (BX, S, S, T)], wide,
    )
    g8, g8a, g8b = call(
        cone_kernel, "cone",
        [coup, v2, ea, eb, own_inv, halo, crit, src, sc, h, ha, hb, pa2, pb2],
        [plane, tile, tile], [(2, 2, S, S, T), (2, S, S, T)],
    )
    eb5, ea5 = swap_b(eb5), swap_a(ea5)
    g8, g8a, g8b = hop(g8, g8a, g8b)
    (out,) = call(
        third_kernel, "third",
        [coup, v5, ea5, eb5, own_inv, halo, crit, src, h, ha, hb, g8, g8a, g8b],
        [field], wide + [(BX, S, OWN), pltpu.SemaphoreType.DMA((BX,))], pltpu.HBM,
    )
    return out


def solution(mesh):
    return jax.shard_map(
        shards,
        mesh=mesh,
        in_specs=(P("flow", None, "gy"), P("flow", None, "gy"), P("flow", None, None, "gy"), P()),
        out_specs=P("flow", None, "gy"),
        check_vma=False,
    )
```

```python
import functools

import jax
import jax.numpy as jnp
from jax import lax
from jax.experimental import pallas as pl
from jax.experimental.pallas import tpu as pltpu
from jax.sharding import PartitionSpec as P

S = 16
BX = 16
CZ = 32
OWN = 512
T = 128
F32 = jnp.float32
BF16 = jnp.bfloat16

SV0 = 6 * 256
PAY1 = SV0 + 18 * S
SV1 = 5 * 256
PAY2 = SV1 + 2 * S
PACK_LIMIT = 58
TURN_LIMIT = 40


def position():
    at = lax.axis_index("gy")
    return lax.axis_index("flow"), at % 2, at == 0, at == lax.axis_size("gy") - 1


def slot_iota(rows):
    return lax.broadcasted_iota(jnp.int32, (rows, T), 1) // CZ


def plane_of(flow, d):
    return jnp.where(flow == 1, d, BX - 1 - d)


def split_couplings(c):
    hi = c.astype(BF16)
    lo = (c - hi.astype(F32)).astype(BF16)
    return jnp.concatenate([hi, hi, lo], axis=1)


def mm(cb, v):
    hi = v.astype(BF16)
    lo = (v - hi.astype(F32)).astype(BF16)
    return jnp.dot(cb, jnp.concatenate([hi, lo, hi], axis=0), preferred_element_type=F32)


def z_masks(width):
    z = lax.broadcasted_iota(jnp.int32, (S, width), 1) % CZ
    return z != 0, z != CZ - 1


def yz_terms(u1, u2, masks):
    width = u1.shape[1]
    below, above = masks
    y = pltpu.roll(u1, CZ, 1) + pltpu.roll(u1, width - CZ, 1)
    z = jnp.where(below, pltpu.roll(u2, 1, 1), 0.0) + jnp.where(above, pltpu.roll(u2, width - 1, 1), 0.0)
    return y + z


def apply_inverse(pieces):
    out = []
    for get, c in pieces:
        acc = get(0) * c[0:1, :]
        for s in range(1, S):
            acc = acc + get(s) * c[s : s + 1, :]
        out.append(acc)
    return out


def low_high(slots, right, left):
    return jnp.where(slots < 2, right, left)


def pack_kernel(state, src, inv, pa1, pb1, pa2, pb2, edge, next1, se, re, s1, s2, sem, osem):
    flow, odd, _, _ = position()
    place = (1 - odd, odd)
    started = []

    def fetch(source, target):
        c = pltpu.make_async_copy(source, target, sem.at[len(started)])
        c.start()
        started.append(c)
        return c

    field = [fetch(x.at[:, :, pl.ds(384 * side, T)], y.at[side]) for x, y in ((state, se), (src, re)) for side in (0, 1)]
    planes = {}
    for d in range(2, BX):
        for side in (0, 1):
            planes[d, side] = fetch(inv.at[plane_of(flow, d), :, pl.ds(384 * side, T)], edge.at[2 * d - 4 + side])
    rest = []
    for side in (0, 1):
        at = pl.ds(384 * side, T)
        at2 = pl.ds(T + T * side, T)
        rest.append(fetch(inv.at[plane_of(flow, 1), :, at2], next1.at[side]))
        rest.append(fetch(inv.at[plane_of(flow, 0), :, at], s1.at[place[side], pl.ds(0, 256)]))
        rest.append(fetch(inv.at[plane_of(flow, 1), :, at], s1.at[place[side], pl.ds(256, 256)]))
        rest.append(fetch(inv.at[plane_of(flow, 0), :, at2], s2.at[place[side], pl.ds(0, 256)]))
        rest.append(fetch(src.at[plane_of(flow, 0), :, at2], s2.at[place[side], pl.ds(SV1, S)]))
    sent = []

    def send(scratch, outs, row, count):
        for j in range(2):
            c = pltpu.make_async_copy(
                scratch.at[j, pl.ds(row, count)], outs[j].at[pl.ds(row, count)], osem.at[len(sent)]
            )
            c.start()
            sent.append(c)

    for c in field:
        c.wait()
    slots = slot_iota(S)
    for side in (0, 1):
        j = place[side]
        row = SV0
        for d in range(BX):
            p = plane_of(flow, d)
            v, r = se[side, p], re[side, p]
            if d < 2:
                s1[j, row : row + S] = v
                s1[j, row + S : row + 2 * S] = r
                row += 2 * S
            else:
                s1[j, row : row + S] = jnp.where((slots >= 2) if side else (slots < 2), v, pltpu.roll(r, 64, 1))
                row += S
        s2[j, SV1 + S : SV1 + 2 * S] = re[side, plane_of(flow, 2)]
    send(s1, (pa1, pb1), SV0, 18 * S)

    slots8 = slot_iota(8)
    for grp in range(3):
        for q in range(4):
            for side in (0, 1):
                planes[2 + 4 * grp + q, side].wait()

        def rows(i, _, grp=grp):
            at = pl.multiple_of(i * 8, 8)
            for side in (0, 1):
                one = two = None
                for q in range(4):
                    x = edge[2 * (4 * grp + q) + side, pl.ds(at, 8), :]
                    x = pltpu.roll(x, CZ * q, 1) if q else x
                    one = x if one is None else jnp.where(slots8 == ((3 if side else 0) + q) % 4, x, one)
                    two = x if two is None else jnp.where(slots8 == ((2 if side else 1) + q) % 4, x, two)
                s1[place[side], pl.ds((2 + grp) * 256 + at, 8), :] = one
                s2[place[side], pl.ds((2 + grp) * 256 + at, 8), :] = two
            return 0

        lax.fori_loop(0, 32, rows, 0, unroll=8)
        send(s1, (pa1, pb1), (2 + grp) * 256, 256)
        send(s2, (pa2, pb2), (2 + grp) * 256, 256)
    for d in (14, 15):
        for side in (0, 1):
            planes[d, side].wait()
    for c in rest:
        c.wait()
    send(s1, (pa1, pb1), 0, 512)
    send(s2, (pa2, pb2), 0, 256)

    def rows(i, _):
        at = pl.multiple_of(i * 8, 8)
        for side in (0, 1):
            j = place[side]
            a = edge[24 + side, pl.ds(at, 8), :]
            b = edge[26 + side, pl.ds(at, 8), :]
            s1[j, pl.ds(5 * 256 + at, 8), :] = jnp.where((slots8 >= 2) if side else (slots8 < 2), a, pltpu.roll(b, 64, 1))
            s2[j, pl.ds(256 + at, 8), :] = jnp.where(
                slots8 == (3 if side else 0), next1[side, pl.ds(at, 8), :], edge[side, pl.ds(at, 8), :]
            )
        return 0

    lax.fori_loop(0, 32, rows, 0, unroll=8)
    send(s1, (pa1, pb1), 5 * 256, 256)
    send(s2, (pa2, pb2), 256, 256)
    send(s2, (pa2, pb2), SV1, 2 * S)
    for c in sent:
        c.wait()


def pack(state, src, inv):
    f = jax.ShapeDtypeStruct
    hbm = pl.BlockSpec(memory_space=pltpu.HBM)
    return pl.pallas_call(
        pack_kernel,
        in_specs=[hbm] * 3,
        out_specs=[hbm] * 4,
        out_shape=[f((PAY1, T), F32)] * 2 + [f((PAY2, T), F32)] * 2,
        scratch_shapes=[
            pltpu.VMEM((2 * BX - 4, 256, T), F32),
            pltpu.VMEM((2, 256, T), F32),
            pltpu.VMEM((2, BX, S, T), F32),
            pltpu.VMEM((2, BX, S, T), F32),
            pltpu.VMEM((2, PAY1, T), F32),
            pltpu.VMEM((2, PAY2, T), F32),
            pltpu.SemaphoreType.DMA((42,)),
            pltpu.SemaphoreType.DMA((24,)),
        ],
        compiler_params=pltpu.CompilerParams(vmem_limit_bytes=PACK_LIMIT * 2**20),
        name="pack",
    )(state, src, inv)


def turn_kernel(inv, out, buf, sem):
    flow = position()[0]

    def copy(i):
        d, tile = i // 4, i % 4
        return pltpu.make_async_copy(
            inv.at[plane_of(flow, d), :, pl.ds(tile * T, T)], buf.at[i], sem.at[d]
        )

    for i in range(4 * BX):
        copy(i).start()
    for d in range(BX):
        for tile in range(4):
            copy(4 * d + tile).wait()
        for tile in range(4):
            for s in range(S):
                out[d, s, :, tile * T : (tile + 1) * T] = buf[4 * d + tile, pl.ds(s, S, stride=S), :]


def turn(inv):
    return pl.pallas_call(
        turn_kernel,
        in_specs=[pl.BlockSpec(memory_space=pltpu.HBM)],
        out_specs=pl.BlockSpec(memory_space=pltpu.VMEM),
        out_shape=jax.ShapeDtypeStruct((BX, S, S, OWN), F32),
        scratch_shapes=[pltpu.VMEM((4 * BX, 256, T), F32), pltpu.SemaphoreType.DMA((BX,))],
        compiler_params=pltpu.CompilerParams(vmem_limit_bytes=TURN_LIMIT * 2**20),
        name="turn",
    )(inv)


def all_planes(cb, width_in, width_out, near, v, u0, u12, src, own_inv, halo_inv, store):
    u0[0, :, :width_in] = jnp.zeros((S, width_in), F32) if near is None else mm(cb, near[:, :width_in])[:S]
    for d in range(BX):
        u = mm(cb, v[d, :, :width_in])
        u0[d + 1, :, :width_in] = u[:S]
        u12[d, :, :width_in] = u[S:]
    masks = z_masks(width_in)
    slots = slot_iota(S)
    for d in range(BX):
        c = yz_terms(u12[d, :S, :width_in], u12[d, S:, :width_in], masks) + u0[d, :, :width_in]
        if d + 1 < BX:
            c = c + u0[d + 2, :, :width_in]
        pieces = [(lambda s, d=d: own_inv[d, s], c[:, :OWN] + src[d, :, :OWN])]
        if width_out > OWN:
            ch = c[:, OWN : OWN + T]
            if width_in == OWN + 2 * T:
                ch = low_high(slots, ch, c[:, OWN + T :])
            pieces.append((lambda s, d=d: halo_inv[d, s], ch + src[d, :, OWN:]))
        for at, x in zip((0, OWN), apply_inverse(pieces)):
            store(d, at, x)


def fit(x, width):
    have = x.shape[1]
    if have == width:
        return x
    side = (width - OWN) // 2
    if side == 0:
        return x[:, :OWN]
    return jnp.concatenate([x[:, : OWN + side], x[:, have - side :]], axis=1)


def crit_step(cb, planes, v, near_u0, src, inv, wide=(), bare=None):
    u = {d: mm(cb, x) for d, x in v.items()}
    out = {}
    for d in planes:
        width = OWN if d == bare else OWN + (4 if d in wide else 2) * T
        parts = []
        if d in u:
            masks = z_masks(u[d].shape[1])
            parts.append(yz_terms(u[d][S : 2 * S], u[d][2 * S :], masks))
        if d == 0:
            parts.append(near_u0)
        elif d - 1 in u:
            parts.append(u[d - 1][:S])
        if d + 1 in u:
            parts.append(u[d + 1][:S])
        if src is not None:
            parts.append(src(d))
        c = functools.reduce(lambda a, b: a + b, [fit(x, width) for x in parts])
        order = (0,) if d == bare else (0, 1, 2, -2, -1) if d in wide else (0, 1, -1)
        pieces = []
        at = 0
        for i in order:
            n = T if i else OWN
            pieces.append((inv(d, i), c[:, at : at + n]))
            at += n
        out[d] = jnp.concatenate(apply_inverse(pieces), axis=1)
    return out


def sides(a, b):
    _, odd, first, last = position()
    right = jnp.where(odd == 1, b, a)
    left = jnp.where(odd == 1, a, b)
    return jnp.where(last, 0.0, right), jnp.where(first, 0.0, left)


def put_edges(x, pa, pb, at, first=0, count=1):
    odd = position()[1]
    low = x[:, first * T : (first + count) * T]
    high = x[:, OWN - (first + count) * T : OWN - first * T]
    pa[at] = jnp.where(odd == 1, low, high)
    pb[at] = jnp.where(odd == 1, high, low)


def first_kernel(
    coup, state, src_in, own_inv, pa1, pb1, g, ga, gb,
    v2, ea, eb, h, ha, hb, halo_inv, crit_inv, src, sc,
    v, vc, u0, u12,
):
    flow = position()[0]
    cb = split_couplings(coup[...])
    slots = slot_iota(S)

    for s in range(S):
        for d in range(2):
            r, l = sides(pa1[pl.ds(d * 256 + s, S, stride=S), :], pb1[pl.ds(d * 256 + s, S, stride=S), :])
            crit_inv[d, 0, s] = r
            crit_inv[d, 1, s] = l
            halo_inv[d, s] = low_high(slots, r, l)
    for grp in range(3):
        for s in range(S):
            at = (2 + grp) * 256 + s
            r, l = sides(pa1[pl.ds(at, S, stride=S), :], pb1[pl.ds(at, S, stride=S), :])
            for q in range(4):
                x = jnp.where(slots == q, r, jnp.where(slots == (q + 3) % 4, l, 0.0))
                halo_inv[2 + 4 * grp + q, s] = pltpu.roll(x, T - CZ * q, 1) if q else x
    for s in range(S):
        at = 5 * 256 + s
        r, l = sides(pa1[pl.ds(at, S, stride=S), :], pb1[pl.ds(at, S, stride=S), :])
        halo_inv[14, s] = low_high(slots, r, l)
        halo_inv[15, s] = pltpu.roll(low_high(slots, l, r), 64, 1)

    for d in range(BX):
        p = plane_of(flow, d)
        v[d, :, :OWN] = state[p]
        src[d, :, :OWN] = src_in[p]
        if d < 2:
            at = SV0 + 2 * S * d
            r, l = sides(pa1[at : at + S], pb1[at : at + S])
            vc[d, :, :T] = r
            vc[d, :, T:] = l
            v[d, :, OWN:] = low_high(slots, r, l)
            r, l = sides(pa1[at + S : at + 2 * S], pb1[at + S : at + 2 * S])
            sc[d, :, :T] = r
            sc[d, :, T:] = l
            src[d, :, OWN:] = low_high(slots, r, l)
        else:
            at = SV0 + 2 * S + S * d
            r, l = sides(pa1[at : at + S], pb1[at : at + S])
            v[d, :, OWN:] = low_high(slots, r, l)
            src[d, :, OWN:] = pltpu.roll(low_high(slots, l, r), 64, 1)

    g_right, g_left = sides(ga[...], gb[...])
    use = flow == 0

    @pl.when(use)
    def _():
        def wide(own, combined, tiles, d):
            if d < 2:
                return jnp.concatenate([own, tiles[d]], axis=1)
            return jnp.concatenate([own, combined, combined], axis=1)

        def inv(d, i):
            if i == 0:
                return lambda s: own_inv[d, s]
            return (lambda s: crit_inv[d, int(i < 0), s]) if d < 2 else (lambda s: halo_inv[d, s])

        vals = {d: wide(v[d, :, :OWN], v[d, :, OWN:], vc, d) for d in range(5)}
        near = mm(cb, jnp.concatenate([g[...], g_right, g_left], axis=1))[:S]
        for k in range(1, 5):
            vals = crit_step(
                cb, range(5 - k), vals, near, lambda d: wide(src[d, :, :OWN], src[d, :, OWN:], sc, d), inv, (), 4 - k
            )
        top = vals[0][:, :OWN]
        h[...] = top
        put_edges(top, ha, hb, slice(None), 0, 2)

    @pl.when(jnp.logical_not(use))
    def _():
        h[...] = jnp.zeros((S, OWN), F32)
        ha[...] = jnp.zeros((S, 2 * T), F32)
        hb[...] = jnp.zeros((S, 2 * T), F32)

    near = jnp.concatenate([g[...], low_high(slots, g_right, g_left)], axis=1)
    near = jnp.where(use, near, 0.0)

    def keep(d, at, x):
        v[d, :, at : at + x.shape[1]] = x

    def final(d, at, x):
        v2[d] = x
        put_edges(x, ea, eb, d)
        if d < 2:
            put_edges(x, ea, eb, BX + d, 1)

    all_planes(cb, 640, 640, near, v, u0, u12, src, own_inv, halo_inv, keep)
    all_planes(cb, 640, 512, near, v, u0, u12, src, own_inv, halo_inv, final)


def load_field(v, v_in, ea_in, eb_in):
    for d in range(BX):
        v[d, :, :OWN] = v_in[d]
        r, l = sides(ea_in[d], eb_in[d])
        v[d, :, OWN : OWN + T] = r
        v[d, :, OWN + T :] = l


def narrow(x, slots):
    x = fit(x, OWN + 2 * T)
    return jnp.concatenate([x[:, :OWN], low_high(slots, x[:, OWN : OWN + T], x[:, OWN + T :])], axis=1)


def second_kernel(
    coup, v_in, ea_in, eb_in, own_inv, halo_in, crit_inv, src, g, ga, gb, h, ha, hb, pa2, pb2,
    v_out, ea, eb, halo_inv,
    v, u0, u12,
):
    flow = position()[0]
    cb = split_couplings(coup[...])
    slots = slot_iota(S)
    load_field(v, v_in, ea_in, eb_in)

    def taken(at):
        return sides(pa2[pl.ds(at, S, stride=S), :], pb2[pl.ds(at, S, stride=S), :])

    for d in (0, 1, 14, 15):
        halo_inv[d] = halo_in[d]
    for grp in range(3):
        for s in range(S):
            r, l = taken((2 + grp) * 256 + s)
            for q in range(4):
                d = 2 + 4 * grp + q
                x = jnp.where(slots == (q + 1) % 4, r, jnp.where(slots == (q + 2) % 4, l, 0.0))
                halo_inv[d, s] = halo_in[d, s] + (pltpu.roll(x, T - CZ * q, 1) if q else x)

    h_wide = jnp.concatenate([h[...], *sides(ha[...], hb[...])], axis=1)

    @pl.when(flow == 1)
    def _():
        def inv(d, i):
            return (lambda s: crit_inv[d, int(i < 0), s]) if i else (lambda s: own_inv[d, s])

        near = mm(cb, fit(h_wide, OWN + 2 * T))[:S]
        d1 = crit_step(cb, range(1), {}, near, None, inv)
        d2 = crit_step(cb, range(2), d1, near, None, inv)
        for d in range(2):
            v[d] = v[d] + d2[d]

    h_near = jnp.where(flow == 1, fit(h_wide, OWN + 2 * T), 0.0)
    g_wide = jnp.concatenate([g[...], *sides(ga[...], gb[...])], axis=1)
    near = jnp.where(flow == 1, h_near, g_wide)

    def keep(d, at, x):
        v[d, :, at : at + x.shape[1]] = x

    def final(d, at, x):
        v_out[d] = x
        put_edges(x, ea, eb, d)

    all_planes(cb, 768, 640, near, v, u0, u12, src, own_inv, halo_inv, keep)
    all_planes(cb, 640, 640, narrow(near, slots), v, u0, u12, src, own_inv, halo_inv, keep)
    all_planes(cb, 640, 512, narrow(h_near, slots), v, u0, u12, src, own_inv, halo_inv, final)


def cone_kernel(
    coup, v_in, ea_in, eb_in, own_inv, halo_inv, crit_inv, src, sc, h, ha, hb, pa2, pb2,
    g8, g8a, g8b,
    far, third,
):
    flow = position()[0]
    cb = split_couplings(coup[...])
    slots = slot_iota(S)

    def taken(at):
        return sides(pa2[pl.ds(at, S, stride=S), :], pb2[pl.ds(at, S, stride=S), :])

    h_wide = jnp.concatenate([h[...], *sides(ha[...], hb[...])], axis=1)

    @pl.when(flow == 1)
    def _():
        for s in range(S):
            far[0, 0, s], far[0, 1, s] = taken(s)
            r, l = taken(256 + s)
            far[1, 0, s] = jnp.where(slots == 0, r, 0.0)
            far[1, 1, s] = jnp.where(slots == 3, l, 0.0)
            third[0, s] = jnp.where(slots < 2, halo_inv[2, s], jnp.where(slots == 2, r, 0.0))
            third[1, s] = jnp.where(slots >= 2, halo_inv[2, s], jnp.where(slots == 1, l, 0.0))

        def inv(d, i):
            if i == 0:
                return lambda s: own_inv[d, s]
            if abs(i) == 2:
                return lambda s: far[d, int(i < 0), s]
            if d < 2:
                return lambda s: crit_inv[d, int(i < 0), s]
            return (lambda s: third[int(i < 0), s]) if d == 2 else (lambda s: halo_inv[d, s])

        near = mm(cb, h_wide)[:S]
        d1 = crit_step(cb, range(1), {}, near, None, inv, (0,))
        d2 = crit_step(cb, range(2), d1, near, None, inv, (0, 1))
        vals = {}
        for d in range(7):
            r, l = sides(ea_in[d], eb_in[d])
            if d < 2:
                r2, l2 = sides(ea_in[BX + d], eb_in[BX + d])
                vals[d] = jnp.concatenate([v_in[d], r, r2, l2, l], axis=1) + d2[d]
            else:
                vals[d] = jnp.concatenate([v_in[d], r, l], axis=1)

        def source(d):
            own = src[d, :, :OWN]
            if d > 2:
                return jnp.concatenate([own, src[d, :, OWN:], src[d, :, OWN:]], axis=1)
            if d == 2:
                return jnp.concatenate([own, *sides(pa2[SV1 + S : SV1 + 2 * S], pb2[SV1 + S : SV1 + 2 * S])], axis=1)
            if d == 1:
                return jnp.concatenate([own, sc[1]], axis=1)
            r, l = sides(pa2[SV1 : SV1 + S], pb2[SV1 : SV1 + S])
            return jnp.concatenate([own, sc[0, :, :T], r, l, sc[0, :, T:]], axis=1)

        for k in range(3, 9):
            vals = crit_step(cb, range(9 - k), vals, near, source, inv, (0,) if k == 3 else (), 8 - k)
        top = vals[0][:, :OWN]
        g8[...] = top
        put_edges(top, g8a, g8b, slice(None))

    @pl.when(flow == 0)
    def _():
        g8[...] = jnp.zeros((S, OWN), F32)
        g8a[...] = jnp.zeros((S, T), F32)
        g8b[...] = jnp.zeros((S, T), F32)


def third_kernel(
    coup, v_in, ea_in, eb_in, own_inv, halo_inv, crit_inv, src, h, ha, hb, g8, g8a, g8b,
    out,
    v, u0, u12, done, sem,
):
    flow = position()[0]
    cb = split_couplings(coup[...])
    slots = slot_iota(S)
    load_field(v, v_in, ea_in, eb_in)
    g_wide = jnp.concatenate([g8[...], *sides(g8a[...], g8b[...])], axis=1)

    @pl.when(flow == 0)
    def _():
        def inv(d, i):
            return (lambda s: crit_inv[d, int(i < 0), s]) if i else (lambda s: own_inv[d, s])

        v[0] = v[0] + crit_step(cb, range(1), {}, mm(cb, g_wide)[:S], None, inv)[0]

    h_wide = fit(jnp.concatenate([h[...], *sides(ha[...], hb[...])], axis=1), OWN + 2 * T)
    near = jnp.where(flow == 1, h_wide, g_wide)

    def keep(d, at, x):
        v[d, :, at : at + x.shape[1]] = x

    sent = []

    def final(d, at, x):
        done[d] = x
        c = pltpu.make_async_copy(done.at[d], out.at[plane_of(flow, d)], sem.at[d])
        c.start()
        sent.append(c)

    all_planes(cb, 768, 640, near, v, u0, u12, src, own_inv, halo_inv, keep)
    all_planes(cb, 640, 640, narrow(near, slots), v, u0, u12, src, own_inv, halo_inv, keep)
    all_planes(cb, 640, 512, narrow(near, slots), v, u0, u12, src, own_inv, halo_inv, final)
    for c in sent:
        c.wait()


def call(kernel, name, ins, outs, scratch, out_space=pltpu.VMEM, limit=16):
    f = jax.ShapeDtypeStruct
    vm = pl.BlockSpec(memory_space=pltpu.VMEM)
    return pl.pallas_call(
        kernel,
        in_specs=[vm] * len(ins),
        out_specs=[pl.BlockSpec(memory_space=out_space)] * len(outs),
        out_shape=[f(s, F32) for s in outs],
        scratch_shapes=[pltpu.VMEM(s, F32) if isinstance(s, tuple) else s for s in scratch],
        compiler_params=pltpu.CompilerParams(vmem_limit_bytes=limit * 2**20),
        name=name,
    )(*ins)


def shards(state, src_in, inverse, couplings):
    count = lax.axis_size("gy")
    flow = lax.axis_index("flow")
    at = lax.axis_index("gy")
    coup = couplings.reshape(3 * S, S)
    inv = inverse.reshape(BX, S * S, OWN)

    mate = [i ^ 1 for i in range(count)]
    other = [(i + 1) % count if i % 2 else (i - 1) % count for i in range(count)]

    def swap_a(x):
        return lax.ppermute(x, "gy", list(enumerate(mate)))

    def swap_b(x):
        return lax.ppermute(x, "gy", list(enumerate(other)))

    def cross(x, to):
        pairs = [(f * count + i, (1 - f) * count + to[i]) for f in (0, 1) for i in range(count)]
        return lax.ppermute(x, ("flow", "gy"), pairs)

    def swap_f(x):
        return lax.ppermute(x, "flow", [(0, 1), (1, 0)])

    def hop(x, xa, xb):
        return swap_f(x), cross(xa, mate), cross(xb, other)

    g = jnp.where(flow == 1, state[0], state[BX - 1])
    low, high = g[:, :T], g[:, OWN - T :]
    ga, gb = jnp.where(at % 2 == 1, low, high), jnp.where(at % 2 == 1, high, low)
    g, ga, gb = hop(g, ga, gb)
    pa1, pb1, pa2, pb2 = pack(state, src_in, inv)
    pb1, pa1 = swap_b(pb1), swap_a(pa1)
    own_inv = turn(inv)
    pa1, g, ga, gb, own_inv, pa2, pb2 = lax.optimization_barrier((pa1, g, ga, gb, own_inv, pa2, pb2))
    pb2, pa2 = swap_b(pb2), swap_a(pa2)

    plane, tile, tiles = (S, OWN), (S, T), (BX, S, T)
    field = (BX, S, OWN)
    v2, ea, eb, h, ha, hb, halo, crit, src, sc = call(
        first_kernel, "first",
        [coup, state, src_in, own_inv, pa1, pb1, g, ga, gb],
        [field, (BX + 2, S, T), (BX + 2, S, T), plane, (S, 2 * T), (S, 2 * T), (BX, S, S, T), (2, 2, S, S, T),
         (BX, S, 640), (2, S, 2 * T)],
        [(BX, S, 640), (2, S, 2 * T), (BX + 2, S, 640), (BX, 2 * S, 640)],
    )
    h, ha, hb, ea, eb, pa2 = lax.optimization_barrier((h, ha, hb, ea, eb, pa2))
    eb, ea = swap_b(eb), swap_a(ea)
    h, ha = swap_f(h), cross(ha, mate)
    ea, hb = lax.optimization_barrier((ea, hb))
    hb = cross(hb, other)
    wide = [(BX, S, 768), (BX + 2, S, 768), (BX, 2 * S, 768)]
    v5, ea5, eb5, halo = call(
        second_kernel, "second",
        [coup, v2, ea, eb, own_inv, halo, crit, src, g, ga, gb, h, ha, hb, pa2, pb2],
        [field, tiles, tiles, (BX, S, S, T)], wide,
    )
    g8, g8a, g8b = call(
        cone_kernel, "cone",
        [coup, v2, ea, eb, own_inv, halo, crit, src, sc, h, ha, hb, pa2, pb2],
        [plane, tile, tile], [(2, 2, S, S, T), (2, S, S, T)],
    )
    eb5, ea5 = swap_b(eb5), swap_a(ea5)
    g8, g8a, g8b = hop(g8, g8a, g8b)
    (out,) = call(
        third_kernel, "third",
        [coup, v5, ea5, eb5, own_inv, halo, crit, src, h, ha, hb, g8, g8a, g8b],
        [field], wide + [(BX, S, OWN), pltpu.SemaphoreType.DMA((BX,))], pltpu.HBM,
    )
    return out


def solution(mesh):
    return jax.shard_map(
        shards,
        mesh=mesh,
        in_specs=(P("flow", None, "gy"), P("flow", None, "gy"), P("flow", None, None, "gy"), P()),
        out_specs=P("flow", None, "gy"),
        check_vma=False,
    )
```
